512 devices in a mesh: fsdp: 64 (over y, z), rep: 8 (over x, core).
Axes of the slice: x: 4, y: 4, z: 16, core: 2. Of those that a mesh axis runs over, the one named last changes fastest.
Arguments:
- grads: bfloat16 [512, 512, 512], P('rep', 'fsdp'), may hold values from -8 to 8
- left_state: bfloat16 [1024, 512, 512], P(('fsdp', 'rep')), may hold values from -1.203125 to 120
- right_state: bfloat16 [1024, 512, 512], P(('fsdp', 'rep')), may hold values from -1.203125 to 120
- block_owner: int32 [512], replicated, may hold values from 0 to 1023, as said below
Outputs:
- update: bfloat16 [512, 512, 512], P('rep', 'fsdp')
- left_new: bfloat16 [1024, 512, 512], P(('fsdp', 'rep'))
- right_new: bfloat16 [1024, 512, 512], P(('fsdp', 'rep'))
The draws below stay inside these ranges and needn't reach their ends.
Inputs may be any that keep to these rules, and one draw needn't show every extreme that they name: `block_owner`: each entry is a slot number: the device's index along fsdp+rep (fsdp index times 8 plus rep index) times 2 plus the slot on that device. No two blocks share a slot. Block b is held by rep index b // 64; for every pair of rep indices g and c exactly 8 of the blocks held by g are owned by devices of rep index c. A device owns 0, 1 or 2 blocks, and in every draw some device owns 2. Where the device at fsdp index f owns two blocks, the device at fsdp index f XOR 64 / 2 with the same rep index owns none.
All inputs are finite; a program needn't handle non-finite values.
Results may differ from the reference program's by a relative error of at most 0.0086.
Values may be sent and summed in bfloat16 or wider, within the bound.
No kernel may reach another device: no remote copies, remote signals or barrier semaphores. Data moves between devices by JAX's collectives and lax.ppermute only.
A program may use at most 64 MiB of HBM per device.

```python
import math
import jax
import jax.numpy as jnp
from jax import lax

B = 512
ITERS = 2
SLOTS = 2
BPG = 64
NB = 512
SLOT_ALL = 1024
N_FSDP = 64
N_REP = 8


def draw_grads(key, part):
    key = jax.random.fold_in(key, 11)
    keys = jax.random.split(key, 3)
    noise = jax.random.normal(keys[0], (NB, B, B), jnp.float32)
    column_scale = jnp.exp(jax.random.uniform(keys[2], (NB, 1, B), jnp.float32, -1.2, 1.2))
    row_scale = jnp.exp(jax.random.uniform(keys[1], (NB, B, 1), jnp.float32, -1.2, 1.2))
    values = noise * row_scale * column_scale
    return jnp.clip(values, -8.0, 8.0).astype(jnp.bfloat16)


def factor_draw(key, lower, upper):
    keys = jax.random.split(key, 2)
    noise = jax.random.uniform(keys[0], (SLOT_ALL, B, B), jnp.float32, -1.2, 1.2)
    mixed = 0.5 * (noise + jnp.swapaxes(noise, 1, 2))
    diagonal = jnp.exp(jax.random.uniform(keys[1], (SLOT_ALL, B, 1), jnp.float32, math.log(lower), math.log(upper)))
    identity = jnp.eye(B, dtype=jnp.float32)
    return (mixed * (1.0 - identity) + diagonal * identity).astype(jnp.bfloat16)


def draw_left_state(key, part):
    key = jax.random.fold_in(key, 21)
    return factor_draw(key, 30.0, 90.0)


def draw_right_state(key, part):
    key = jax.random.fold_in(key, 31)
    return factor_draw(key, 30.0, 90.0)


def draw_block_owner(key, part):
    key = jax.random.fold_in(key, 41)
    half_count = N_FSDP // 2
    share = BPG // N_REP
    doubles = BPG // 4
    singles = BPG - 2 * doubles
    group_perms = [jax.random.permutation(jax.random.fold_in(key, 1000 + group), BPG) for group in range(N_REP)]
    owner = jnp.zeros((NB,), jnp.int32)
    for column in range(N_REP):
        column_key = jax.random.fold_in(key, column)
        pairs = jax.random.permutation(jax.random.fold_in(column_key, 1), half_count).astype(jnp.int32)
        sides = jax.random.randint(jax.random.fold_in(column_key, 2), (doubles,), 0, 2).astype(jnp.int32)
        double_devices = pairs[:doubles] + sides * half_count
        single_pairs = pairs[doubles:doubles + singles // 2]
        single_devices = jnp.concatenate([single_pairs, single_pairs + half_count])
        single_slots = jax.random.randint(jax.random.fold_in(column_key, 3), (singles,), 0, SLOTS).astype(jnp.int32)
        places = jnp.concatenate([jnp.repeat(double_devices, 2), single_devices])
        slot_pick = jnp.concatenate([jnp.tile(jnp.arange(2, dtype=jnp.int32), doubles), single_slots])
        slot_ids = (places * N_REP + column) * SLOTS + slot_pick
        chosen = jnp.concatenate([group * BPG + group_perms[group][column * share:(column + 1) * share].astype(jnp.int32) for group in range(N_REP)])
        shuffle = jax.random.permutation(jax.random.fold_in(column_key, 4), BPG)
        owner = owner.at[chosen[shuffle]].set(slot_ids)
    return owner


def setup_inputs(seed: int = 0) -> dict:
    key_of = jax.random.split(jax.random.key(seed), 5)
    return {
        "grads": draw_grads(jax.random.fold_in(key_of[4], 71), 0),
        "left_state": draw_left_state(jax.random.fold_in(key_of[4], 71), 0),
        "right_state": draw_right_state(jax.random.fold_in(key_of[4], 71), 0),
        "block_owner": draw_block_owner(jax.random.fold_in(key_of[4], 71), 0),
    }


DECAY_RATE = 0.95

def multiply(first, second):
    return jnp.dot(first, second, preferred_element_type=jnp.float32)

def inverse_root(stored):
    factor = stored.astype(jnp.float32)
    scaling = 2.5 / jnp.sqrt(jnp.sum(factor * factor))
    current = scaling * factor
    identity = jnp.eye(factor.shape[0], dtype=jnp.float32)
    result = current.astype(jnp.bfloat16)
    for iteration in range(ITERS):
        tangent = ((5.0 * identity - current) * 0.25).astype(jnp.bfloat16)
        if iteration == 0:
            result = tangent
        else:
            result = multiply(result, tangent).astype(jnp.bfloat16)
        if iteration + 1 < ITERS:
            square = multiply(tangent, tangent).astype(jnp.bfloat16)
            fourth = multiply(square, square).astype(jnp.bfloat16)
            current = multiply(fourth, current.astype(jnp.bfloat16))
    return result

def refresh(old_left, old_right, gradient):
    left_gram = lax.dot_general(gradient, gradient, (((1,), (1,)), ((), ())), preferred_element_type=jnp.float32)
    right_gram = lax.dot_general(gradient, gradient, (((0,), (0,)), ((), ())), preferred_element_type=jnp.float32)
    left_factor = (DECAY_RATE * old_left.astype(jnp.float32) + (1.0 - DECAY_RATE) * left_gram).astype(jnp.bfloat16)
    right_factor = (DECAY_RATE * old_right.astype(jnp.float32) + (1.0 - DECAY_RATE) * right_gram).astype(jnp.bfloat16)
    return (left_factor, right_factor)

def precondition(left_factor, right_factor, gradient):
    half_product = multiply(inverse_root(left_factor), gradient).astype(jnp.bfloat16)
    raw_update = multiply(half_product, inverse_root(right_factor))
    wide = gradient.astype(jnp.float32)
    grad_norm = jnp.sqrt(jnp.sum(wide * wide))
    raw_norm = jnp.sqrt(jnp.sum(raw_update * raw_update))
    return (raw_update * (grad_norm / (raw_norm + 1e-06))).astype(jnp.bfloat16)

def reference(grads, left_state, right_state, block_owner):

    def one_block(block_index):
        slot_id = block_owner[block_index]
        gradient = grads[block_index]
        left_factor, right_factor = refresh(left_state[slot_id], right_state[slot_id], gradient)
        return (left_factor, right_factor, precondition(left_factor, right_factor, gradient))
    left_parts, right_parts, update = lax.map(one_block, jnp.arange(block_owner.shape[0], dtype=jnp.int32))
    left_new = left_state.at[block_owner].set(left_parts)
    right_new = right_state.at[block_owner].set(right_parts)
    return (update, left_new, right_new)
```

```python
import jax
import jax.numpy as jnp
from jax import lax
from jax.experimental import pallas as pl
from jax.experimental.pallas import tpu as pltpu
from jax.sharding import PartitionSpec as P

ITERS = 2
DECAY_RATE = 0.95
VMEM_LIMIT = 32 * 1024 * 1024


def multiply(first, second):
    return jnp.dot(first, second, preferred_element_type=jnp.float32)


def inverse_root(stored):
    factor = stored.astype(jnp.float32)
    scaling = 2.5 / jnp.sqrt(jnp.sum(factor * factor))
    current = scaling * factor
    width = factor.shape[0]
    rows = lax.broadcasted_iota(jnp.int32, (width, width), 0)
    columns = lax.broadcasted_iota(jnp.int32, (width, width), 1)
    five = jnp.where(rows == columns, 5.0, 0.0)
    result = None
    for iteration in range(ITERS):
        tangent = ((five - current) * 0.25).astype(jnp.bfloat16)
        if iteration == 0:
            result = tangent
        else:
            result = multiply(result, tangent).astype(jnp.bfloat16)
        if iteration + 1 < ITERS:
            square = multiply(tangent, tangent).astype(jnp.bfloat16)
            fourth = multiply(square, square).astype(jnp.bfloat16)
            current = multiply(fourth, current.astype(jnp.bfloat16))
    return result


def block_kernel(
    choice, gradient_ref, left_own, right_own, left_lent, right_lent,
    update_ref, left_ref, right_ref, left_old, right_old, sems,
):
    lent, slot = choice[0], choice[1]

    @pl.when(lent == 1)
    def _():
        pltpu.make_async_copy(left_lent, left_old, sems.at[0]).start()
        pltpu.make_async_copy(right_lent, right_old, sems.at[1]).start()

    @pl.when(lent == 0)
    def _():
        pltpu.make_async_copy(left_own.at[slot], left_old, sems.at[0]).start()
        pltpu.make_async_copy(right_own.at[slot], right_old, sems.at[1]).start()

    pltpu.make_async_copy(left_lent, left_old, sems.at[0]).wait()
    pltpu.make_async_copy(right_lent, right_old, sems.at[1]).wait()
    gradient = gradient_ref[...]
    left_gram = lax.dot_general(
        gradient, gradient, (((1,), (1,)), ((), ())), preferred_element_type=jnp.float32
    )
    left_factor = (
        DECAY_RATE * left_old[...].astype(jnp.float32) + (1.0 - DECAY_RATE) * left_gram
    ).astype(jnp.bfloat16)
    left_ref[...] = left_factor
    right_gram = lax.dot_general(
        gradient, gradient, (((0,), (0,)), ((), ())), preferred_element_type=jnp.float32
    )
    right_factor = (
        DECAY_RATE * right_old[...].astype(jnp.float32) + (1.0 - DECAY_RATE) * right_gram
    ).astype(jnp.bfloat16)
    right_ref[...] = right_factor
    left_root = inverse_root(left_factor)
    right_root = inverse_root(right_factor)
    half_product = multiply(left_root, gradient).astype(jnp.bfloat16)
    raw_update = multiply(half_product, right_root)
    wide = gradient.astype(jnp.float32)
    grad_norm = jnp.sqrt(jnp.sum(wide * wide))
    raw_norm = jnp.sqrt(jnp.sum(raw_update * raw_update))
    update_ref[...] = (raw_update * (grad_norm / (raw_norm + 1e-06))).astype(jnp.bfloat16)


def work_on_block(choice, gradient, left_state, right_state, left_lent, right_lent):
    width = gradient.shape[0]
    square = jax.ShapeDtypeStruct((width, width), jnp.bfloat16)
    return pl.pallas_call(
        block_kernel,
        out_shape=(square, square, square),
        in_specs=[
            pl.BlockSpec(memory_space=pltpu.SMEM),
            pl.BlockSpec(memory_space=pltpu.VMEM),
        ]
        + [pl.BlockSpec(memory_space=pl.ANY)] * 4,
        out_specs=[pl.BlockSpec(memory_space=pltpu.VMEM)] * 3,
        scratch_shapes=[
            pltpu.VMEM((width, width), jnp.bfloat16),
            pltpu.VMEM((width, width), jnp.bfloat16),
            pltpu.SemaphoreType.DMA((2,)),
        ],
        compiler_params=pltpu.CompilerParams(vmem_limit_bytes=VMEM_LIMIT),
        cost_estimate=pl.CostEstimate(
            flops=24 * width**3, bytes_accessed=12 * width**2, transcendentals=0
        ),
        name="block_step",
    )(choice, gradient, left_state, right_state, left_lent, right_lent)


def pick(array, order):
    return array.at[order].get(mode="promise_in_bounds", unique_indices=True)


def local(grads, left_state, right_state, block_owner):
    rep_count = lax.axis_size("rep")
    fsdp_count = lax.axis_size("fsdp")
    group_index = lax.axis_index("rep")
    place_index = lax.axis_index("fsdp")
    held_blocks, shard_rows, block_width = grads.shape
    column_share = held_blocks // rep_count
    slot_count = left_state.shape[0]
    half = fsdp_count // 2
    swap = [(place, place ^ half) for place in range(fsdp_count)]
    positions = jnp.arange(held_blocks, dtype=jnp.int32)

    left_lent = lax.ppermute(left_state[1], "fsdp", swap)
    right_lent = lax.ppermute(right_state[1], "fsdp", swap)

    owner_table = block_owner.reshape(rep_count, held_blocks)
    owner_column = owner_table // slot_count % rep_count
    before = positions[None, :] < positions[:, None]

    my_column = lax.dynamic_index_in_dim(owner_column, group_index, 0, keepdims=False)
    alike = (my_column[:, None] == my_column[None, :]) & before
    my_order = my_column * column_share + jnp.sum(alike.astype(jnp.int32), axis=1)
    my_picked = jnp.sum(
        jnp.where(my_order[None, :] == positions[:, None], positions[None, :], 0), axis=1
    )
    arrived = lax.all_to_all(
        pick(grads, my_picked), "rep", split_axis=0, concat_axis=0, tiled=True
    )

    mine = owner_column == group_index
    rank = jnp.sum((mine[:, None, :] & before[None]).astype(jnp.int32), axis=2)
    shares = jnp.arange(column_share, dtype=jnp.int32)
    taken = mine[:, None, :] & (rank[:, None, :] == shares[None, :, None])
    entry_owner = jnp.sum(jnp.where(taken, owner_table[:, None, :], 0), axis=2).reshape(-1)

    sibling = jnp.any(entry_owner[None, :] == entry_owner[:, None] - 1, axis=1)
    second = (entry_owner % slot_count == 1) & sibling
    owner_place = entry_owner // (slot_count * rep_count)
    worker = jnp.where(second, owner_place ^ half, owner_place)
    source_entry = jnp.sum(
        jnp.where(worker[None, :] == positions[:, None], positions[None, :], 0), axis=1
    )
    gradient = lax.all_to_all(
        pick(arrived, source_entry), "fsdp", split_axis=0, concat_axis=0, tiled=True
    ).reshape(fsdp_count * shard_rows, block_width)

    first_slot = (place_index * rep_count + group_index) * slot_count
    owns_first = jnp.any(entry_owner == first_slot)
    owns_second = jnp.any(entry_owner == first_slot + 1)
    lent = ~(owns_first | owns_second)
    choice = jnp.stack([lent, ~owns_first]).astype(jnp.int32)
    update_block, left_done, right_done = work_on_block(
        choice, gradient, left_state, right_state, left_lent, right_lent
    )

    returned_rows = lax.all_to_all(
        update_block.reshape(fsdp_count, shard_rows, block_width),
        "fsdp", split_axis=0, concat_axis=0, tiled=True,
    )
    left_back = lax.ppermute(left_done, "fsdp", swap)
    right_back = lax.ppermute(right_done, "fsdp", swap)
    at_home = lax.all_to_all(
        pick(returned_rows, worker), "rep", split_axis=0, concat_axis=0, tiled=True
    )
    update = pick(at_home, my_order)

    def settled(state, done, back):
        first = jnp.where(owns_first, done, state[0])
        other = jnp.where(owns_first, back, done)
        return jnp.stack([first, jnp.where(owns_second, other, state[1])])

    return (
        update,
        settled(left_state, left_done, left_back),
        settled(right_state, right_done, right_back),
    )


def solution(mesh):
    return jax.shard_map(
        local,
        mesh=mesh,
        in_specs=(
            P("rep", "fsdp", None),
            P(("fsdp", "rep"), None, None),
            P(("fsdp", "rep"), None, None),
            P(),
        ),
        out_specs=(
            P("rep", "fsdp", None),
            P(("fsdp", "rep"), None, None),
            P(("fsdp", "rep"), None, None),
        ),
        check_vma=False,
    )
```

```python
import jax
import jax.numpy as jnp
from jax import lax
from jax.experimental import pallas as pl
from jax.experimental.pallas import tpu as pltpu
from jax.sharding import PartitionSpec as P

ITERS = 2
DECAY_RATE = 0.95
VMEM_LIMIT = 32 * 1024 * 1024


def multiply(first, second):
    return jnp.dot(first, second, preferred_element_type=jnp.float32)


def inverse_root(stored):
    factor = stored.astype(jnp.float32)
    scaling = 2.5 / jnp.sqrt(jnp.sum(factor * factor))
    current = scaling * factor
    width = factor.shape[0]
    rows = lax.broadcasted_iota(jnp.int32, (width, width), 0)
    columns = lax.broadcasted_iota(jnp.int32, (width, width), 1)
    five = jnp.where(rows == columns, 5.0, 0.0)
    result = None
    for iteration in range(ITERS):
        tangent = ((five - current) * 0.25).astype(jnp.bfloat16)
        if iteration == 0:
            result = tangent
        else:
            result = multiply(result, tangent).astype(jnp.bfloat16)
        if iteration + 1 < ITERS:
            square = multiply(tangent, tangent).astype(jnp.bfloat16)
            fourth = multiply(square, square).astype(jnp.bfloat16)
            current = multiply(fourth, current.astype(jnp.bfloat16))
    return result


def new_factors(gradient, left_old, right_old):
    left_gram = lax.dot_general(
        gradient, gradient, (((1,), (1,)), ((), ())), preferred_element_type=jnp.float32
    )
    left_factor = (
        DECAY_RATE * left_old.astype(jnp.float32) + (1.0 - DECAY_RATE) * left_gram
    ).astype(jnp.bfloat16)
    right_gram = lax.dot_general(
        gradient, gradient, (((0,), (0,)), ((), ())), preferred_element_type=jnp.float32
    )
    right_factor = (
        DECAY_RATE * right_old.astype(jnp.float32) + (1.0 - DECAY_RATE) * right_gram
    ).astype(jnp.bfloat16)
    return left_factor, right_factor


def block_kernel(
    choice, gradient_ref, left_own, right_own, lent_early, lent_late,
    update_out, left_out, right_out, gradient_out,
    left_old, right_old, left_new, right_new, update, old_sems, out_sems, update_sems,
):
    lent, slot = choice[0], choice[1]
    width = left_old.shape[0]
    early = lent_early.shape[0]

    @pl.when(lent == 1)
    def _():
        pltpu.make_async_copy(lent_early, left_old.at[:early], old_sems.at[0]).start()
        pltpu.make_async_copy(
            lent_late.at[: width - early], left_old.at[early:], old_sems.at[1]
        ).start()
        pltpu.make_async_copy(
            lent_late.at[width - early :], right_old, old_sems.at[2]
        ).start()

    @pl.when(lent == 0)
    def _():
        pltpu.make_async_copy(
            left_own.at[slot, :early], left_old.at[:early], old_sems.at[0]
        ).start()
        pltpu.make_async_copy(
            left_own.at[slot, early:], left_old.at[early:], old_sems.at[1]
        ).start()
        pltpu.make_async_copy(right_own.at[slot], right_old, old_sems.at[2]).start()

    keep_gradient = pltpu.make_async_copy(gradient_ref, gradient_out, out_sems.at[2])
    keep_gradient.start()
    pltpu.make_async_copy(lent_early, left_old.at[:early], old_sems.at[0]).wait()
    pltpu.make_async_copy(
        lent_late.at[: width - early], left_old.at[early:], old_sems.at[1]
    ).wait()
    pltpu.make_async_copy(lent_late.at[width - early :], right_old, old_sems.at[2]).wait()
    gradient = gradient_ref[...]
    left_factor, right_factor = new_factors(gradient, left_old[...], right_old[...])
    left_new[...] = left_factor
    right_new[...] = right_factor
    keep_left = pltpu.make_async_copy(left_new, left_out, out_sems.at[0])
    keep_right = pltpu.make_async_copy(right_new, right_out, out_sems.at[1])
    keep_left.start()
    keep_right.start()
    left_root = inverse_root(left_factor)
    right_root = inverse_root(right_factor)
    half_product = multiply(left_root, gradient).astype(jnp.bfloat16)
    raw_update = multiply(half_product, right_root)
    wide = gradient.astype(jnp.float32)
    grad_norm = jnp.sqrt(jnp.sum(wide * wide))
    raw_norm = jnp.sqrt(jnp.sum(raw_update * raw_update))
    scale = grad_norm / (raw_norm + 1e-06)
    sends = []
    part = width // update_sems.shape[0]
    for number in range(update_sems.shape[0]):
        rows = slice(number * part, (number + 1) * part)
        update[rows, :] = (raw_update[rows, :] * scale).astype(jnp.bfloat16)
        send = pltpu.make_async_copy(
            update.at[rows], update_out.at[rows], update_sems.at[number]
        )
        send.start()
        sends.append(send)
    for send in [keep_gradient, keep_left, keep_right] + sends:
        send.wait()


def work_on_block(choice, gradient, left_state, right_state, lent_early, lent_late):
    width = gradient.shape[0]
    square = pltpu.HBM((width, width), jnp.bfloat16)
    return pl.pallas_call(
        block_kernel,
        out_shape=(square,) * 4,
        in_specs=[
            pl.BlockSpec(memory_space=pltpu.SMEM),
            pl.BlockSpec(memory_space=pltpu.VMEM),
        ]
        + [pl.BlockSpec(memory_space=pl.ANY)] * 4,
        out_specs=[pl.BlockSpec(memory_space=pltpu.HBM)] * 4,
        scratch_shapes=[pltpu.VMEM((width, width), jnp.bfloat16)] * 5
        + [pltpu.SemaphoreType.DMA((3,)), pltpu.SemaphoreType.DMA((3,)), pltpu.SemaphoreType.DMA((4,))],
        compiler_params=pltpu.CompilerParams(vmem_limit_bytes=VMEM_LIMIT),
        cost_estimate=pl.CostEstimate(
            flops=24 * width**3, bytes_accessed=12 * width**2, transcendentals=0
        ),
        name="block_step",
    )(choice, gradient, left_state, right_state, lent_early, lent_late)


def settle_kernel(
    choice, gradient_back, left_own, right_own, left_done, right_done, left_out, right_out,
    gradient, left, right, sems,
):
    has_first, has_second = choice[2] == 1, choice[3] == 1
    has_both = has_first & has_second

    @pl.when(has_first)
    def _():
        pltpu.make_async_copy(left_done, left_out.at[0], sems.at[0]).start()
        pltpu.make_async_copy(right_done, right_out.at[0], sems.at[1]).start()

    @pl.when(~has_first)
    def _():
        pltpu.make_async_copy(left_own.at[0], left_out.at[0], sems.at[0]).start()
        pltpu.make_async_copy(right_own.at[0], right_out.at[0], sems.at[1]).start()

    @pl.when(has_second & ~has_first)
    def _():
        pltpu.make_async_copy(left_done, left_out.at[1], sems.at[2]).start()
        pltpu.make_async_copy(right_done, right_out.at[1], sems.at[3]).start()

    @pl.when(~has_second)
    def _():
        pltpu.make_async_copy(left_own.at[1], left_out.at[1], sems.at[2]).start()
        pltpu.make_async_copy(right_own.at[1], right_out.at[1], sems.at[3]).start()

    @pl.when(has_both)
    def _():
        loads = [
            pltpu.make_async_copy(left_own.at[1], left, sems.at[2]),
            pltpu.make_async_copy(right_own.at[1], right, sems.at[3]),
            pltpu.make_async_copy(gradient_back, gradient, sems.at[4]),
        ]
        for load in loads:
            load.start()
        for load in loads:
            load.wait()
        left_factor, right_factor = new_factors(gradient[...], left[...], right[...])
        left[...] = left_factor
        right[...] = right_factor
        pltpu.make_async_copy(left, left_out.at[1], sems.at[2]).start()
        pltpu.make_async_copy(right, right_out.at[1], sems.at[3]).start()

    for number, (source, target) in enumerate(
        [(left_done, left_out.at[0]), (right_done, right_out.at[0])]
        + [(left_done, left_out.at[1]), (right_done, right_out.at[1])]
    ):
        pltpu.make_async_copy(source, target, sems.at[number]).wait()


def settle(choice, gradient_back, left_state, right_state, left_done, right_done):
    slots, width, _ = left_state.shape
    both = pltpu.HBM(left_state.shape, jnp.bfloat16)
    return pl.pallas_call(
        settle_kernel,
        out_shape=(both, both),
        in_specs=[pl.BlockSpec(memory_space=pltpu.SMEM)]
        + [pl.BlockSpec(memory_space=pl.ANY)] * 5,
        out_specs=[pl.BlockSpec(memory_space=pltpu.HBM)] * 2,
        scratch_shapes=[pltpu.VMEM((width, width), jnp.bfloat16)] * 3
        + [pltpu.SemaphoreType.DMA((5,))],
        compiler_params=pltpu.CompilerParams(vmem_limit_bytes=VMEM_LIMIT),
        cost_estimate=pl.CostEstimate(
            flops=4 * width**3, bytes_accessed=16 * width**2, transcendentals=0
        ),
        name="settle_slots",
    )(choice, gradient_back, left_state, right_state, left_done, right_done)


def reorder_kernel(order, source, *rest):
    result, sem = rest[-2:]

    def move(number, carry):
        pltpu.make_async_copy(source.at[order[number]], result.at[number], sem).start()
        return carry

    lax.fori_loop(0, result.shape[0], move, 0, unroll=8)
    pltpu.make_async_copy(source, result, sem).wait()


def reorder(array, order, *needed):
    return pl.pallas_call(
        reorder_kernel,
        out_shape=pltpu.HBM(array.shape, array.dtype),
        in_specs=[pl.BlockSpec(memory_space=pltpu.SMEM)]
        + [pl.BlockSpec(memory_space=pl.ANY)] * (1 + len(needed)),
        out_specs=pl.BlockSpec(memory_space=pltpu.HBM),
        scratch_shapes=[pltpu.SemaphoreType.DMA],
        compiler_params=pltpu.CompilerParams(vmem_limit_bytes=VMEM_LIMIT // 4),
        name="reorder",
    )(order, array, *needed)


def local(grads, left_state, right_state, block_owner):
    rep_count = lax.axis_size("rep")
    fsdp_count = lax.axis_size("fsdp")
    group_index = lax.axis_index("rep")
    place_index = lax.axis_index("fsdp")
    held_blocks, shard_rows, block_width = grads.shape
    column_share = held_blocks // rep_count
    slot_count = left_state.shape[0]
    half = fsdp_count // 2
    swap = [(place, place ^ half) for place in range(fsdp_count)]
    positions = jnp.arange(held_blocks, dtype=jnp.int32)

    early = block_width // 2
    lent_early = lax.ppermute(left_state[1, :early], "fsdp", swap)
    lent_late = lax.ppermute(
        jnp.concatenate([left_state[1, early:], right_state[1]]), "fsdp", swap
    )

    owner_table = block_owner.reshape(rep_count, held_blocks)
    owner_column = owner_table // slot_count % rep_count
    before = positions[None, :] < positions[:, None]

    my_column = lax.dynamic_index_in_dim(owner_column, group_index, 0, keepdims=False)
    alike = (my_column[:, None] == my_column[None, :]) & before
    my_order = my_column * column_share + jnp.sum(alike.astype(jnp.int32), axis=1)
    my_picked = jnp.sum(
        jnp.where(my_order[None, :] == positions[:, None], positions[None, :], 0), axis=1
    )
    arrived = lax.all_to_all(
        reorder(pltpu.with_memory_space_constraint(grads, pltpu.HBM), my_picked),
        "rep", split_axis=0, concat_axis=0, tiled=True,
    )

    mine = owner_column == group_index
    rank = jnp.sum((mine[:, None, :] & before[None]).astype(jnp.int32), axis=2)
    shares = jnp.arange(column_share, dtype=jnp.int32)
    taken = mine[:, None, :] & (rank[:, None, :] == shares[None, :, None])
    entry_owner = jnp.sum(jnp.where(taken, owner_table[:, None, :], 0), axis=2).reshape(-1)

    sibling = jnp.any(entry_owner[None, :] == entry_owner[:, None] - 1, axis=1)
    second = (entry_owner % slot_count == 1) & sibling
    owner_place = entry_owner // (slot_count * rep_count)
    worker = jnp.where(second, owner_place ^ half, owner_place)
    source_entry = jnp.sum(
        jnp.where(worker[None, :] == positions[:, None], positions[None, :], 0), axis=1
    )
    gradient = lax.all_to_all(
        reorder(arrived, source_entry, lent_early),
        "fsdp", split_axis=0, concat_axis=0, tiled=True,
    ).reshape(fsdp_count * shard_rows, block_width)

    first_slot = (place_index * rep_count + group_index) * slot_count
    owns_first = jnp.any(entry_owner == first_slot)
    owns_second = jnp.any(entry_owner == first_slot + 1)
    lent = ~(owns_first | owns_second)
    choice = jnp.stack([lent, ~owns_first, owns_first, owns_second]).astype(jnp.int32)
    update_block, left_done, right_done, gradient = work_on_block(
        choice, gradient, left_state, right_state, lent_early, lent_late
    )

    returned_rows = lax.all_to_all(
        update_block.reshape(fsdp_count, shard_rows, block_width),
        "fsdp", split_axis=0, concat_axis=0, tiled=True,
    )
    gradient_back = lax.ppermute(gradient, "fsdp", swap)
    left_new, right_new = settle(
        choice, gradient_back, left_state, right_state, left_done, right_done
    )
    at_home = lax.all_to_all(
        reorder(returned_rows, worker), "rep", split_axis=0, concat_axis=0, tiled=True
    )
    update = reorder(at_home, my_order)
    return (update, left_new, right_new)


def solution(mesh):
    return jax.shard_map(
        local,
        mesh=mesh,
        in_specs=(
            P("rep", "fsdp", None),
            P(("fsdp", "rep"), None, None),
            P(("fsdp", "rep"), None, None),
            P(),
        ),
        out_specs=(
            P("rep", "fsdp", None),
            P(("fsdp", "rep"), None, None),
            P(("fsdp", "rep"), None, None),
        ),
        check_vma=False,
    )
```

```python
import jax
import jax.numpy as jnp
from jax import lax
from jax.experimental import pallas as pl
from jax.experimental.pallas import tpu as pltpu
from jax.sharding import PartitionSpec as P

ITERS = 2
DECAY_RATE = 0.95
VMEM_LIMIT = 32 * 1024 * 1024
EARLY_ROWS = 448


def multiply(first, second):
    return jnp.dot(first, second, preferred_element_type=jnp.float32)


def inverse_root(stored):
    factor = stored.astype(jnp.float32)
    scaling = 2.5 / jnp.sqrt(jnp.sum(factor * factor))
    current = scaling * factor
    width = factor.shape[0]
    rows = lax.broadcasted_iota(jnp.int32, (width, width), 0)
    columns = lax.broadcasted_iota(jnp.int32, (width, width), 1)
    five = jnp.where(rows == columns, 5.0, 0.0)
    result = None
    for iteration in range(ITERS):
        tangent = ((five - current) * 0.25).astype(jnp.bfloat16)
        if iteration == 0:
            result = tangent
        else:
            result = multiply(result, tangent).astype(jnp.bfloat16)
        if iteration + 1 < ITERS:
            square = multiply(tangent, tangent).astype(jnp.bfloat16)
            fourth = multiply(square, square).astype(jnp.bfloat16)
            current = multiply(fourth, current.astype(jnp.bfloat16))
    return result


def grams(gradient):
    left = lax.dot_general(
        gradient, gradient, (((1,), (1,)), ((), ())), preferred_element_type=jnp.float32
    )
    right = lax.dot_general(
        gradient, gradient, (((0,), (0,)), ((), ())), preferred_element_type=jnp.float32
    )
    return left, right


def blend(old, gram):
    return (
        DECAY_RATE * old.astype(jnp.float32) + (1.0 - DECAY_RATE) * gram
    ).astype(jnp.bfloat16)


def block_kernel(
    choice, gradient_ref, left_own, right_own, lent_early, lent_late,
    update_out, left_out, right_out, gradient_out,
    left_old, right_old, left_new, right_new, update, old_sems, out_sems, update_sems,
):
    lent, slot = choice[0], choice[1]
    width = left_old.shape[0]
    early = lent_early.shape[0]

    @pl.when(lent == 1)
    def _():
        pltpu.make_async_copy(lent_early, left_old.at[:early], old_sems.at[0]).start()
        pltpu.make_async_copy(
            lent_late.at[: width - early], left_old.at[early:], old_sems.at[1]
        ).start()
        pltpu.make_async_copy(
            lent_late.at[width - early :], right_old, old_sems.at[2]
        ).start()

    @pl.when(lent == 0)
    def _():
        pltpu.make_async_copy(
            left_own.at[slot, :early], left_old.at[:early], old_sems.at[0]
        ).start()
        pltpu.make_async_copy(
            left_own.at[slot, early:], left_old.at[early:], old_sems.at[1]
        ).start()
        pltpu.make_async_copy(right_own.at[slot], right_old, old_sems.at[2]).start()

    keep_gradient = pltpu.make_async_copy(gradient_ref, gradient_out, out_sems.at[2])
    keep_gradient.start()
    pltpu.make_async_copy(lent_early, left_old.at[:early], old_sems.at[0]).wait()
    pltpu.make_async_copy(
        lent_late.at[: width - early], left_old.at[early:], old_sems.at[1]
    ).wait()
    pltpu.make_async_copy(lent_late.at[width - early :], right_old, old_sems.at[2]).wait()
    gradient = gradient_ref[...]
    left_gram, right_gram = grams(gradient)
    left_factor = blend(left_old[...], left_gram)
    right_factor = blend(right_old[...], right_gram)
    left_new[...] = left_factor
    right_new[...] = right_factor
    keep_left = pltpu.make_async_copy(left_new, left_out, out_sems.at[0])
    keep_right = pltpu.make_async_copy(right_new, right_out, out_sems.at[1])
    keep_left.start()
    keep_right.start()
    left_root = inverse_root(left_factor)
    right_root = inverse_root(right_factor)
    half_product = multiply(left_root, gradient).astype(jnp.bfloat16)
    raw_update = multiply(half_product, right_root)
    wide = gradient.astype(jnp.float32)
    grad_norm = jnp.sqrt(jnp.sum(wide * wide))
    raw_norm = jnp.sqrt(jnp.sum(raw_update * raw_update))
    scale = grad_norm / (raw_norm + 1e-06)
    sends = []
    part = width // update_sems.shape[0]
    for number in range(update_sems.shape[0]):
        rows = slice(number * part, (number + 1) * part)
        update[rows, :] = (raw_update[rows, :] * scale).astype(jnp.bfloat16)
        send = pltpu.make_async_copy(
            update.at[rows], update_out.at[rows], update_sems.at[number]
        )
        send.start()
        sends.append(send)
    for send in [keep_gradient, keep_left, keep_right] + sends:
        send.wait()


def work_on_block(choice, gradient, left_state, right_state, lent_early, lent_late):
    width = gradient.shape[0]
    square = pltpu.HBM((width, width), jnp.bfloat16)
    return pl.pallas_call(
        block_kernel,
        out_shape=(square,) * 4,
        in_specs=[
            pl.BlockSpec(memory_space=pltpu.SMEM),
            pl.BlockSpec(memory_space=pltpu.VMEM),
        ]
        + [pl.BlockSpec(memory_space=pl.ANY)] * 4,
        out_specs=[pl.BlockSpec(memory_space=pltpu.HBM)] * 4,
        scratch_shapes=[pltpu.VMEM((width, width), jnp.bfloat16)] * 5
        + [pltpu.SemaphoreType.DMA((3,)), pltpu.SemaphoreType.DMA((3,)), pltpu.SemaphoreType.DMA((4,))],
        compiler_params=pltpu.CompilerParams(vmem_limit_bytes=VMEM_LIMIT),
        cost_estimate=pl.CostEstimate(
            flops=24 * width**3, bytes_accessed=12 * width**2, transcendentals=0
        ),
        name="block_step",
    )(choice, gradient, left_state, right_state, lent_early, lent_late)


def settle_kernel(
    choice, gradient_back, left_own, right_own, left_done, right_done, left_out, right_out,
    gradient, left, right, sems,
):
    has_first, has_second = choice[2] == 1, choice[3] == 1
    has_both = has_first & has_second

    @pl.when(has_first)
    def _():
        pltpu.make_async_copy(left_done, left_out.at[0], sems.at[0]).start()
        pltpu.make_async_copy(right_done, right_out.at[0], sems.at[1]).start()

    @pl.when(~has_first)
    def _():
        pltpu.make_async_copy(left_own.at[0], left_out.at[0], sems.at[0]).start()
        pltpu.make_async_copy(right_own.at[0], right_out.at[0], sems.at[1]).start()

    @pl.when(has_second & ~has_first)
    def _():
        pltpu.make_async_copy(left_done, left_out.at[1], sems.at[2]).start()
        pltpu.make_async_copy(right_done, right_out.at[1], sems.at[3]).start()

    @pl.when(~has_second)
    def _():
        pltpu.make_async_copy(left_own.at[1], left_out.at[1], sems.at[2]).start()
        pltpu.make_async_copy(right_own.at[1], right_out.at[1], sems.at[3]).start()

    @pl.when(has_both)
    def _():
        loads = [
            pltpu.make_async_copy(left_own.at[1], left, sems.at[2]),
            pltpu.make_async_copy(right_own.at[1], right, sems.at[3]),
            pltpu.make_async_copy(gradient_back, gradient, sems.at[4]),
        ]
        for load in loads:
            load.start()
        for load in loads:
            load.wait()
        left_gram, right_gram = grams(gradient[...])
        left[...] = blend(left[...], left_gram)
        right[...] = blend(right[...], right_gram)
        pltpu.make_async_copy(left, left_out.at[1], sems.at[2]).start()
        pltpu.make_async_copy(right, right_out.at[1], sems.at[3]).start()

    for number, (source, target) in enumerate(
        [(left_done, left_out.at[0]), (right_done, right_out.at[0])]
        + [(left_done, left_out.at[1]), (right_done, right_out.at[1])]
    ):
        pltpu.make_async_copy(source, target, sems.at[number]).wait()


def settle(choice, gradient_back, left_state, right_state, left_done, right_done):
    slots, width, _ = left_state.shape
    both = pltpu.HBM(left_state.shape, jnp.bfloat16)
    return pl.pallas_call(
        settle_kernel,
        out_shape=(both, both),
        in_specs=[pl.BlockSpec(memory_space=pltpu.SMEM)]
        + [pl.BlockSpec(memory_space=pl.ANY)] * 5,
        out_specs=[pl.BlockSpec(memory_space=pltpu.HBM)] * 2,
        scratch_shapes=[pltpu.VMEM((width, width), jnp.bfloat16)] * 3
        + [pltpu.SemaphoreType.DMA((5,))],
        compiler_params=pltpu.CompilerParams(vmem_limit_bytes=VMEM_LIMIT),
        cost_estimate=pl.CostEstimate(
            flops=4 * width**3, bytes_accessed=16 * width**2, transcendentals=0
        ),
        name="settle_slots",
    )(choice, gradient_back, left_state, right_state, left_done, right_done)


def reorder_kernel(order, source, *rest):
    result, sem = rest[-2:]

    def move(number, carry):
        pltpu.make_async_copy(source.at[order[number]], result.at[number], sem).start()
        return carry

    lax.fori_loop(0, result.shape[0], move, 0, unroll=8)
    pltpu.make_async_copy(source, result, sem).wait()


def reorder(array, order, *needed):
    return pl.pallas_call(
        reorder_kernel,
        out_shape=pltpu.HBM(array.shape, array.dtype),
        in_specs=[pl.BlockSpec(memory_space=pltpu.SMEM)]
        + [pl.BlockSpec(memory_space=pl.ANY)] * (1 + len(needed)),
        out_specs=pl.BlockSpec(memory_space=pltpu.HBM),
        scratch_shapes=[pltpu.SemaphoreType.DMA],
        compiler_params=pltpu.CompilerParams(vmem_limit_bytes=VMEM_LIMIT // 4),
        name="reorder",
    )(order, array, *needed)


def late_loan_kernel(left_own, right_own, result, held, sems):
    width = right_own.shape[1]
    rest = held.shape[0] - width
    loads = [
        pltpu.make_async_copy(
            left_own.at[1, width - rest :], held.at[:rest], sems.at[0]
        ),
        pltpu.make_async_copy(right_own.at[1], held.at[rest:], sems.at[1]),
    ]
    for load in loads:
        load.start()
    for load in loads:
        load.wait()
    store = pltpu.make_async_copy(held, result, sems.at[2])
    store.start()
    store.wait()


def late_loan(left_state, right_state, early):
    width = left_state.shape[1]
    shape = (2 * width - early, width)
    return pl.pallas_call(
        late_loan_kernel,
        out_shape=pltpu.HBM(shape, jnp.bfloat16),
        in_specs=[pl.BlockSpec(memory_space=pl.ANY)] * 2,
        out_specs=pl.BlockSpec(memory_space=pltpu.HBM),
        scratch_shapes=[pltpu.VMEM(shape, jnp.bfloat16), pltpu.SemaphoreType.DMA((3,))],
        compiler_params=pltpu.CompilerParams(vmem_limit_bytes=VMEM_LIMIT // 4),
        name="late_loan",
    )(left_state, right_state)


def pick(array, order):
    return array.at[order].get(mode="promise_in_bounds", unique_indices=True)


def local(grads, left_state, right_state, block_owner):
    rep_count = lax.axis_size("rep")
    fsdp_count = lax.axis_size("fsdp")
    group_index = lax.axis_index("rep")
    place_index = lax.axis_index("fsdp")
    held_blocks, shard_rows, block_width = grads.shape
    column_share = held_blocks // rep_count
    slot_count = left_state.shape[0]
    half = fsdp_count // 2
    swap = [(place, place ^ half) for place in range(fsdp_count)]
    positions = jnp.arange(held_blocks, dtype=jnp.int32)

    early = EARLY_ROWS
    lent_early = lax.ppermute(left_state[1, :early], "fsdp", swap)
    lent_late = lax.ppermute(late_loan(left_state, right_state, early), "fsdp", swap)

    owner_table = block_owner.reshape(rep_count, held_blocks)
    owner_column = owner_table // slot_count % rep_count
    before = positions[None, :] < positions[:, None]

    my_column = lax.dynamic_index_in_dim(owner_column, group_index, 0, keepdims=False)
    alike = (my_column[:, None] == my_column[None, :]) & before
    my_order = my_column * column_share + jnp.sum(alike.astype(jnp.int32), axis=1)
    my_picked = jnp.sum(
        jnp.where(my_order[None, :] == positions[:, None], positions[None, :], 0), axis=1
    )
    arrived = lax.all_to_all(
        pick(grads, my_picked),
        "rep", split_axis=0, concat_axis=0, tiled=True,
    )

    mine = owner_column == group_index
    rank = jnp.sum((mine[:, None, :] & before[None]).astype(jnp.int32), axis=2)
    shares = jnp.arange(column_share, dtype=jnp.int32)
    taken = mine[:, None, :] & (rank[:, None, :] == shares[None, :, None])
    entry_owner = jnp.sum(jnp.where(taken, owner_table[:, None, :], 0), axis=2).reshape(-1)

    sibling = jnp.any(entry_owner[None, :] == entry_owner[:, None] - 1, axis=1)
    second = (entry_owner % slot_count == 1) & sibling
    owner_place = entry_owner // (slot_count * rep_count)
    worker = jnp.where(second, owner_place ^ half, owner_place)
    source_entry = jnp.sum(
        jnp.where(worker[None, :] == positions[:, None], positions[None, :], 0), axis=1
    )
    gradient = lax.all_to_all(
        reorder(arrived, source_entry, lent_early),
        "fsdp", split_axis=0, concat_axis=0, tiled=True,
    ).reshape(fsdp_count * shard_rows, block_width)

    first_slot = (place_index * rep_count + group_index) * slot_count
    owns_first = jnp.any(entry_owner == first_slot)
    owns_second = jnp.any(entry_owner == first_slot + 1)
    lent = ~(owns_first | owns_second)
    choice = jnp.stack([lent, ~owns_first, owns_first, owns_second]).astype(jnp.int32)
    update_block, left_done, right_done, gradient = work_on_block(
        choice, gradient, left_state, right_state, lent_early, lent_late
    )

    returned_rows = lax.all_to_all(
        update_block.reshape(fsdp_count, shard_rows, block_width),
        "fsdp", split_axis=0, concat_axis=0, tiled=True,
    )
    gradient_back = lax.ppermute(gradient, "fsdp", swap)
    left_new, right_new = settle(
        choice, gradient_back, left_state, right_state, left_done, right_done
    )
    at_home = lax.all_to_all(
        reorder(returned_rows, worker), "rep", split_axis=0, concat_axis=0, tiled=True
    )
    update = reorder(at_home, my_order)
    return (update, left_new, right_new)


def solution(mesh):
    return jax.shard_map(
        local,
        mesh=mesh,
        in_specs=(
            P("rep", "fsdp", None),
            P(("fsdp", "rep"), None, None),
            P(("fsdp", "rep"), None, None),
            P(),
        ),
        out_specs=(
            P("rep", "fsdp", None),
            P(("fsdp", "rep"), None, None),
            P(("fsdp", "rep"), None, None),
        ),
        check_vma=False,
    )
```

```python
import functools

import jax
import jax.numpy as jnp
from jax import lax
from jax.experimental import pallas as pl
from jax.experimental.pallas import tpu as pltpu
from jax.sharding import PartitionSpec as P

ITERS = 2
DECAY_RATE = 0.95
VMEM_LIMIT = 32 * 1024 * 1024
EARLY_ROWS = 448
REP_ORDER = (3, 6, 0, 5, 7, 1, 4, 2)
FSDP_ORDER = (
    61, 7, 0, 62, 39, 24, 40, 32, 53, 34, 3, 41, 51, 63, 6, 21,
    43, 14, 38, 49, 30, 19, 23, 37, 55, 28, 58, 17, 29, 36, 52, 18,
    22, 54, 57, 50, 5, 56, 31, 27, 60, 12, 2, 8, 48, 4, 46, 44,
    33, 47, 26, 13, 11, 1, 25, 16, 59, 15, 45, 42, 20, 35, 9, 10,
)


def multiply(first, second):
    return jnp.dot(first, second, preferred_element_type=jnp.float32)


def inverse_root(stored):
    factor = stored.astype(jnp.float32)
    scaling = 2.5 / jnp.sqrt(jnp.sum(factor * factor))
    current = scaling * factor
    width = factor.shape[0]
    rows = lax.broadcasted_iota(jnp.int32, (width, width), 0)
    columns = lax.broadcasted_iota(jnp.int32, (width, width), 1)
    five = jnp.where(rows == columns, 5.0, 0.0)
    result = None
    for iteration in range(ITERS):
        tangent = ((five - current) * 0.25).astype(jnp.bfloat16)
        if iteration == 0:
            result = tangent
        else:
            result = multiply(result, tangent).astype(jnp.bfloat16)
        if iteration + 1 < ITERS:
            square = multiply(tangent, tangent).astype(jnp.bfloat16)
            fourth = multiply(square, square).astype(jnp.bfloat16)
            current = multiply(fourth, current.astype(jnp.bfloat16))
    return result


def grams(gradient):
    left = lax.dot_general(
        gradient, gradient, (((1,), (1,)), ((), ())), preferred_element_type=jnp.float32
    )
    right = lax.dot_general(
        gradient, gradient, (((0,), (0,)), ((), ())), preferred_element_type=jnp.float32
    )
    return left, right


def blend(old, gram):
    return (
        DECAY_RATE * old.astype(jnp.float32) + (1.0 - DECAY_RATE) * gram
    ).astype(jnp.bfloat16)


def block_kernel(
    order, choice, shares_ref, left_own, right_own, lent_early, lent_late,
    update_out, left_out, right_out, gradient_out,
    left_old, right_old, left_new, right_new, gradient_ref, update,
    old_sems, out_sems, update_sems,
):
    rows = shares_ref.shape[1]
    lent, slot = choice[0], choice[1]
    width = left_old.shape[0]
    early = lent_early.shape[0]

    @pl.when(lent == 1)
    def _():
        pltpu.make_async_copy(lent_early, left_old.at[:early], old_sems.at[0]).start()
        pltpu.make_async_copy(
            lent_late.at[: width - early], left_old.at[early:], old_sems.at[1]
        ).start()
        pltpu.make_async_copy(
            lent_late.at[width - early :], right_old, old_sems.at[2]
        ).start()

    @pl.when(lent == 0)
    def _():
        pltpu.make_async_copy(
            left_own.at[slot, :early], left_old.at[:early], old_sems.at[0]
        ).start()
        pltpu.make_async_copy(
            left_own.at[slot, early:], left_old.at[early:], old_sems.at[1]
        ).start()
        pltpu.make_async_copy(right_own.at[slot], right_old, old_sems.at[2]).start()

    for number, place in enumerate(order):
        gradient_ref[place * rows : (place + 1) * rows, :] = shares_ref[number]
    keep_gradient = pltpu.make_async_copy(gradient_ref, gradient_out, out_sems.at[2])
    keep_gradient.start()
    pltpu.make_async_copy(lent_early, left_old.at[:early], old_sems.at[0]).wait()
    pltpu.make_async_copy(
        lent_late.at[: width - early], left_old.at[early:], old_sems.at[1]
    ).wait()
    pltpu.make_async_copy(lent_late.at[width - early :], right_old, old_sems.at[2]).wait()
    gradient = gradient_ref[...]
    left_gram, right_gram = grams(gradient)
    left_factor = blend(left_old[...], left_gram)
    right_factor = blend(right_old[...], right_gram)
    left_new[...] = left_factor
    right_new[...] = right_factor
    keep_left = pltpu.make_async_copy(left_new, left_out, out_sems.at[0])
    keep_right = pltpu.make_async_copy(right_new, right_out, out_sems.at[1])
    keep_left.start()
    keep_right.start()
    left_root = inverse_root(left_factor)
    right_root = inverse_root(right_factor)
    half_product = multiply(left_root, gradient).astype(jnp.bfloat16)
    raw_update = multiply(half_product, right_root)
    wide = gradient.astype(jnp.float32)
    grad_norm = jnp.sqrt(jnp.sum(wide * wide))
    raw_norm = jnp.sqrt(jnp.sum(raw_update * raw_update))
    scale = grad_norm / (raw_norm + 1e-06)
    sends = []
    part = len(order) // update_sems.shape[0]
    for number in range(update_sems.shape[0]):
        shares = slice(number * part, (number + 1) * part)
        for share in range(number * part, (number + 1) * part):
            place = order[share]
            piece = raw_update[place * rows : (place + 1) * rows, :]
            update[share] = (piece * scale).astype(jnp.bfloat16)
        send = pltpu.make_async_copy(
            update.at[shares], update_out.at[shares], update_sems.at[number]
        )
        send.start()
        sends.append(send)
    for send in [keep_gradient, keep_left, keep_right] + sends:
        send.wait()


def work_on_block(
    order, choice, shares, left_state, right_state, lent_early, lent_late
):
    width = shares.shape[2]
    square = pltpu.HBM((width, width), jnp.bfloat16)
    return pl.pallas_call(
        functools.partial(block_kernel, order),
        out_shape=(pltpu.HBM(shares.shape, jnp.bfloat16),) + (square,) * 3,
        in_specs=[
            pl.BlockSpec(memory_space=pltpu.SMEM),
            pl.BlockSpec(memory_space=pltpu.VMEM),
        ]
        + [pl.BlockSpec(memory_space=pl.ANY)] * 4,
        out_specs=[pl.BlockSpec(memory_space=pltpu.HBM)] * 4,
        scratch_shapes=[pltpu.VMEM((width, width), jnp.bfloat16)] * 5
        + [pltpu.VMEM(shares.shape, jnp.bfloat16)]
        + [pltpu.SemaphoreType.DMA((3,)), pltpu.SemaphoreType.DMA((3,)), pltpu.SemaphoreType.DMA((4,))],
        compiler_params=pltpu.CompilerParams(vmem_limit_bytes=VMEM_LIMIT),
        cost_estimate=pl.CostEstimate(
            flops=24 * width**3, bytes_accessed=12 * width**2, transcendentals=0
        ),
        name="block_step",
    )(choice, shares, left_state, right_state, lent_early, lent_late)


def settle_kernel(
    choice, gradient_back, left_own, right_own, left_done, right_done, left_out, right_out,
    gradient, left, right, sems,
):
    has_first, has_second = choice[2] == 1, choice[3] == 1
    has_both = has_first & has_second

    @pl.when(has_first)
    def _():
        pltpu.make_async_copy(left_done, left_out.at[0], sems.at[0]).start()
        pltpu.make_async_copy(right_done, right_out.at[0], sems.at[1]).start()

    @pl.when(~has_first)
    def _():
        pltpu.make_async_copy(left_own.at[0], left_out.at[0], sems.at[0]).start()
        pltpu.make_async_copy(right_own.at[0], right_out.at[0], sems.at[1]).start()

    @pl.when(has_second & ~has_first)
    def _():
        pltpu.make_async_copy(left_done, left_out.at[1], sems.at[2]).start()
        pltpu.make_async_copy(right_done, right_out.at[1], sems.at[3]).start()

    @pl.when(~has_second)
    def _():
        pltpu.make_async_copy(left_own.at[1], left_out.at[1], sems.at[2]).start()
        pltpu.make_async_copy(right_own.at[1], right_out.at[1], sems.at[3]).start()

    @pl.when(has_both)
    def _():
        loads = [
            pltpu.make_async_copy(left_own.at[1], left, sems.at[2]),
            pltpu.make_async_copy(right_own.at[1], right, sems.at[3]),
            pltpu.make_async_copy(gradient_back, gradient, sems.at[4]),
        ]
        for load in loads:
            load.start()
        for load in loads:
            load.wait()
        left_gram, right_gram = grams(gradient[...])
        left[...] = blend(left[...], left_gram)
        right[...] = blend(right[...], right_gram)
        pltpu.make_async_copy(left, left_out.at[1], sems.at[2]).start()
        pltpu.make_async_copy(right, right_out.at[1], sems.at[3]).start()

    for number, (source, target) in enumerate(
        [(left_done, left_out.at[0]), (right_done, right_out.at[0])]
        + [(left_done, left_out.at[1]), (right_done, right_out.at[1])]
    ):
        pltpu.make_async_copy(source, target, sems.at[number]).wait()


def settle(choice, gradient_back, left_state, right_state, left_done, right_done):
    slots, width, _ = left_state.shape
    both = pltpu.HBM(left_state.shape, jnp.bfloat16)
    return pl.pallas_call(
        settle_kernel,
        out_shape=(both, both),
        in_specs=[pl.BlockSpec(memory_space=pltpu.SMEM)]
        + [pl.BlockSpec(memory_space=pl.ANY)] * 5,
        out_specs=[pl.BlockSpec(memory_space=pltpu.HBM)] * 2,
        scratch_shapes=[pltpu.VMEM((width, width), jnp.bfloat16)] * 3
        + [pltpu.SemaphoreType.DMA((5,))],
        compiler_params=pltpu.CompilerParams(vmem_limit_bytes=VMEM_LIMIT),
        cost_estimate=pl.CostEstimate(
            flops=4 * width**3, bytes_accessed=16 * width**2, transcendentals=0
        ),
        name="settle_slots",
    )(choice, gradient_back, left_state, right_state, left_done, right_done)


def reorder_kernel(order, source, *rest):
    result, sem = rest[-2:]

    def move(number, carry):
        pltpu.make_async_copy(source.at[order[number]], result.at[number], sem).start()
        return carry

    lax.fori_loop(0, result.shape[0], move, 0, unroll=8)
    pltpu.make_async_copy(source, result, sem).wait()


def reorder(array, order, *needed):
    return pl.pallas_call(
        reorder_kernel,
        out_shape=pltpu.HBM(array.shape, array.dtype),
        in_specs=[pl.BlockSpec(memory_space=pltpu.SMEM)]
        + [pl.BlockSpec(memory_space=pl.ANY)] * (1 + len(needed)),
        out_specs=pl.BlockSpec(memory_space=pltpu.HBM),
        scratch_shapes=[pltpu.SemaphoreType.DMA],
        compiler_params=pltpu.CompilerParams(vmem_limit_bytes=VMEM_LIMIT // 4),
        name="reorder",
    )(order, array, *needed)


def late_loan_kernel(left_own, right_own, result, held, sems):
    width = right_own.shape[1]
    rest = held.shape[0] - width
    loads = [
        pltpu.make_async_copy(
            left_own.at[1, width - rest :], held.at[:rest], sems.at[0]
        ),
        pltpu.make_async_copy(right_own.at[1], held.at[rest:], sems.at[1]),
    ]
    for load in loads:
        load.start()
    for load in loads:
        load.wait()
    store = pltpu.make_async_copy(held, result, sems.at[2])
    store.start()
    store.wait()


def late_loan(left_state, right_state, early):
    width = left_state.shape[1]
    shape = (2 * width - early, width)
    return pl.pallas_call(
        late_loan_kernel,
        out_shape=pltpu.HBM(shape, jnp.bfloat16),
        in_specs=[pl.BlockSpec(memory_space=pl.ANY)] * 2,
        out_specs=pl.BlockSpec(memory_space=pltpu.HBM),
        scratch_shapes=[pltpu.VMEM(shape, jnp.bfloat16), pltpu.SemaphoreType.DMA((3,))],
        compiler_params=pltpu.CompilerParams(vmem_limit_bytes=VMEM_LIMIT // 4),
        name="late_loan",
    )(left_state, right_state)


def exchange_order(order, count):
    if len(order) != count:
        order = tuple(range(count))
    places = [order.index(device) for device in range(count)]
    return [list(order)], places


def pick(array, order):
    return array.at[order].get(mode="promise_in_bounds", unique_indices=True)


def local(grads, left_state, right_state, block_owner):
    rep_count = lax.axis_size("rep")
    fsdp_count = lax.axis_size("fsdp")
    group_index = lax.axis_index("rep")
    place_index = lax.axis_index("fsdp")
    held_blocks, shard_rows, block_width = grads.shape
    column_share = held_blocks // rep_count
    slot_count = left_state.shape[0]
    half = fsdp_count // 2
    swap = [(place, place ^ half) for place in range(fsdp_count)]
    positions = jnp.arange(held_blocks, dtype=jnp.int32)

    early = EARLY_ROWS
    lent_early = lax.ppermute(left_state[1, :early], "fsdp", swap)
    lent_late = lax.ppermute(late_loan(left_state, right_state, early), "fsdp", swap)

    rep_groups, rep_place = exchange_order(REP_ORDER, rep_count)
    fsdp_groups, fsdp_place = exchange_order(FSDP_ORDER, fsdp_count)
    owner_table = block_owner.reshape(rep_count, held_blocks)
    owner_column = owner_table // slot_count % rep_count
    before = positions[None, :] < positions[:, None]

    my_column = lax.dynamic_index_in_dim(owner_column, group_index, 0, keepdims=False)
    alike = (my_column[:, None] == my_column[None, :]) & before
    my_place = sum(jnp.where(my_column == c, rep_place[c], 0) for c in range(rep_count))
    my_order = my_place * column_share + jnp.sum(alike.astype(jnp.int32), axis=1)
    my_picked = jnp.sum(
        jnp.where(my_order[None, :] == positions[:, None], positions[None, :], 0), axis=1
    )
    arrived = lax.all_to_all(
        pick(grads, my_picked),
        "rep", split_axis=0, concat_axis=0, tiled=True,
        axis_index_groups=rep_groups,
    )

    arrival_table = jnp.stack([owner_table[group] for group in rep_groups[0]])
    mine = arrival_table // slot_count % rep_count == group_index
    rank = jnp.sum((mine[:, None, :] & before[None]).astype(jnp.int32), axis=2)
    shares = jnp.arange(column_share, dtype=jnp.int32)
    taken = mine[:, None, :] & (rank[:, None, :] == shares[None, :, None])
    entry_owner = jnp.sum(jnp.where(taken, arrival_table[:, None, :], 0), axis=2).reshape(-1)

    sibling = jnp.any(entry_owner[None, :] == entry_owner[:, None] - 1, axis=1)
    second = (entry_owner % slot_count == 1) & sibling
    owner_place = entry_owner // (slot_count * rep_count)
    worker = jnp.where(second, owner_place ^ half, owner_place)
    worker_place = jnp.sum(
        jnp.where(
            worker[:, None] == jnp.array(fsdp_groups[0], jnp.int32)[None, :],
            positions[None, :], 0,
        ),
        axis=1,
    )
    source_entry = jnp.sum(
        jnp.where(worker_place[None, :] == positions[:, None], positions[None, :], 0), axis=1
    )
    gradient = lax.all_to_all(
        reorder(arrived, source_entry, lent_early),
        "fsdp", split_axis=0, concat_axis=0, tiled=True,
        axis_index_groups=fsdp_groups,
    )

    first_slot = (place_index * rep_count + group_index) * slot_count
    owns_first = jnp.any(entry_owner == first_slot)
    owns_second = jnp.any(entry_owner == first_slot + 1)
    lent = ~(owns_first | owns_second)
    choice = jnp.stack([lent, ~owns_first, owns_first, owns_second]).astype(jnp.int32)
    update_block, left_done, right_done, gradient = work_on_block(
        fsdp_groups[0], choice, gradient, left_state, right_state, lent_early, lent_late
    )

    returned_rows = lax.all_to_all(
        update_block,
        "fsdp", split_axis=0, concat_axis=0, tiled=True,
        axis_index_groups=fsdp_groups,
    )
    gradient_back = lax.ppermute(gradient, "fsdp", swap)
    left_new, right_new = settle(
        choice, gradient_back, left_state, right_state, left_done, right_done
    )
    at_home = lax.all_to_all(
        reorder(returned_rows, worker_place), "rep", split_axis=0, concat_axis=0, tiled=True,
        axis_index_groups=rep_groups
    )
    update = reorder(at_home, my_order)
    return (update, left_new, right_new)


def solution(mesh):
    return jax.shard_map(
        local,
        mesh=mesh,
        in_specs=(
            P("rep", "fsdp", None),
            P(("fsdp", "rep"), None, None),
            P(("fsdp", "rep"), None, None),
            P(),
        ),
        out_specs=(
            P("rep", "fsdp", None),
            P(("fsdp", "rep"), None, None),
            P(("fsdp", "rep"), None, None),
        ),
        check_vma=False,
    )
```

```python
import functools

import jax
import jax.numpy as jnp
from jax import lax
from jax.experimental import pallas as pl
from jax.experimental.pallas import tpu as pltpu
from jax.sharding import PartitionSpec as P

ITERS = 2
DECAY_RATE = 0.95
VMEM_LIMIT = 32 * 1024 * 1024
EARLY_ROWS = 448
REP_ORDER = (3, 6, 0, 5, 7, 1, 4, 2)
FSDP_FIRST = 43


def multiply(first, second):
    return jnp.dot(first, second, preferred_element_type=jnp.float32)


def inverse_root(stored):
    factor = stored.astype(jnp.float32)
    scaling = 2.5 / jnp.sqrt(jnp.sum(factor * factor))
    current = scaling * factor
    width = factor.shape[0]
    rows = lax.broadcasted_iota(jnp.int32, (width, width), 0)
    columns = lax.broadcasted_iota(jnp.int32, (width, width), 1)
    five = jnp.where(rows == columns, 5.0, 0.0)
    result = None
    for iteration in range(ITERS):
        tangent = ((five - current) * 0.25).astype(jnp.bfloat16)
        if iteration == 0:
            result = tangent
        else:
            result = multiply(result, tangent).astype(jnp.bfloat16)
        if iteration + 1 < ITERS:
            square = multiply(tangent, tangent).astype(jnp.bfloat16)
            fourth = multiply(square, square).astype(jnp.bfloat16)
            current = multiply(fourth, current.astype(jnp.bfloat16))
    return result


def grams(gradient):
    left = lax.dot_general(
        gradient, gradient, (((1,), (1,)), ((), ())), preferred_element_type=jnp.float32
    )
    right = lax.dot_general(
        gradient, gradient, (((0,), (0,)), ((), ())), preferred_element_type=jnp.float32
    )
    return left, right


def blend(old, gram):
    return (
        DECAY_RATE * old.astype(jnp.float32) + (1.0 - DECAY_RATE) * gram
    ).astype(jnp.bfloat16)


def block_kernel(
    order, choice, shares_ref, left_own, right_own, lent_early, lent_late,
    update_out, left_out, right_out, gradient_out,
    left_old, right_old, left_new, right_new, gradient_ref, update,
    old_sems, out_sems, update_sems,
):
    rows = shares_ref.shape[1]
    lent, slot = choice[0], choice[1]
    width = left_old.shape[0]
    early = lent_early.shape[0]

    @pl.when(lent == 1)
    def _():
        pltpu.make_async_copy(lent_early, left_old.at[:early], old_sems.at[0]).start()
        pltpu.make_async_copy(
            lent_late.at[: width - early], left_old.at[early:], old_sems.at[1]
        ).start()
        pltpu.make_async_copy(
            lent_late.at[width - early :], right_old, old_sems.at[2]
        ).start()

    @pl.when(lent == 0)
    def _():
        pltpu.make_async_copy(
            left_own.at[slot, :early], left_old.at[:early], old_sems.at[0]
        ).start()
        pltpu.make_async_copy(
            left_own.at[slot, early:], left_old.at[early:], old_sems.at[1]
        ).start()
        pltpu.make_async_copy(right_own.at[slot], right_old, old_sems.at[2]).start()

    for number, place in enumerate(order):
        gradient_ref[place * rows : (place + 1) * rows, :] = shares_ref[number]
    keep_gradient = pltpu.make_async_copy(gradient_ref, gradient_out, out_sems.at[2])
    keep_gradient.start()
    pltpu.make_async_copy(lent_early, left_old.at[:early], old_sems.at[0]).wait()
    pltpu.make_async_copy(
        lent_late.at[: width - early], left_old.at[early:], old_sems.at[1]
    ).wait()
    pltpu.make_async_copy(lent_late.at[width - early :], right_old, old_sems.at[2]).wait()
    gradient = gradient_ref[...]
    left_gram, right_gram = grams(gradient)
    left_factor = blend(left_old[...], left_gram)
    right_factor = blend(right_old[...], right_gram)
    left_new[...] = left_factor
    right_new[...] = right_factor
    keep_left = pltpu.make_async_copy(left_new, left_out, out_sems.at[0])
    keep_right = pltpu.make_async_copy(right_new, right_out, out_sems.at[1])
    keep_left.start()
    keep_right.start()
    left_root = inverse_root(left_factor)
    right_root = inverse_root(right_factor)
    half_product = multiply(left_root, gradient).astype(jnp.bfloat16)
    raw_update = multiply(half_product, right_root)
    wide = gradient.astype(jnp.float32)
    grad_norm = jnp.sqrt(jnp.sum(wide * wide))
    raw_norm = jnp.sqrt(jnp.sum(raw_update * raw_update))
    scale = grad_norm / (raw_norm + 1e-06)
    sends = []
    part = len(order) // update_sems.shape[0]
    for number in range(update_sems.shape[0]):
        shares = slice(number * part, (number + 1) * part)
        for share in range(number * part, (number + 1) * part):
            place = order[share]
            piece = raw_update[place * rows : (place + 1) * rows, :]
            update[share] = (piece * scale).astype(jnp.bfloat16)
        send = pltpu.make_async_copy(
            update.at[shares], update_out.at[shares], update_sems.at[number]
        )
        send.start()
        sends.append(send)
    for send in [keep_gradient, keep_left, keep_right] + sends:
        send.wait()


def work_on_block(
    order, choice, shares, left_state, right_state, lent_early, lent_late
):
    width = shares.shape[2]
    square = pltpu.HBM((width, width), jnp.bfloat16)
    return pl.pallas_call(
        functools.partial(block_kernel, order),
        out_shape=(pltpu.HBM(shares.shape, jnp.bfloat16),) + (square,) * 3,
        in_specs=[
            pl.BlockSpec(memory_space=pltpu.SMEM),
            pl.BlockSpec(memory_space=pltpu.VMEM),
        ]
        + [pl.BlockSpec(memory_space=pl.ANY)] * 4,
        out_specs=[pl.BlockSpec(memory_space=pltpu.HBM)] * 4,
        scratch_shapes=[pltpu.VMEM((width, width), jnp.bfloat16)] * 5
        + [pltpu.VMEM(shares.shape, jnp.bfloat16)]
        + [pltpu.SemaphoreType.DMA((3,)), pltpu.SemaphoreType.DMA((3,)), pltpu.SemaphoreType.DMA((4,))],
        compiler_params=pltpu.CompilerParams(vmem_limit_bytes=VMEM_LIMIT),
        cost_estimate=pl.CostEstimate(
            flops=24 * width**3, bytes_accessed=12 * width**2, transcendentals=0
        ),
        name="block_step",
    )(choice, shares, left_state, right_state, lent_early, lent_late)


def settle_kernel(
    choice, gradient_back, left_own, right_own, left_done, right_done, left_out, right_out,
    gradient, left, right, sems,
):
    has_first, has_second = choice[2] == 1, choice[3] == 1
    has_both = has_first & has_second

    @pl.when(has_first)
    def _():
        pltpu.make_async_copy(left_done, left_out.at[0], sems.at[0]).start()
        pltpu.make_async_copy(right_done, right_out.at[0], sems.at[1]).start()

    @pl.when(~has_first)
    def _():
        pltpu.make_async_copy(left_own.at[0], left_out.at[0], sems.at[0]).start()
        pltpu.make_async_copy(right_own.at[0], right_out.at[0], sems.at[1]).start()

    @pl.when(has_second & ~has_first)
    def _():
        pltpu.make_async_copy(left_done, left_out.at[1], sems.at[2]).start()
        pltpu.make_async_copy(right_done, right_out.at[1], sems.at[3]).start()

    @pl.when(~has_second)
    def _():
        pltpu.make_async_copy(left_own.at[1], left_out.at[1], sems.at[2]).start()
        pltpu.make_async_copy(right_own.at[1], right_out.at[1], sems.at[3]).start()

    @pl.when(has_both)
    def _():
        loads = [
            pltpu.make_async_copy(left_own.at[1], left, sems.at[2]),
            pltpu.make_async_copy(right_own.at[1], right, sems.at[3]),
            pltpu.make_async_copy(gradient_back, gradient, sems.at[4]),
        ]
        for load in loads:
            load.start()
        for load in loads:
            load.wait()
        left_gram, right_gram = grams(gradient[...])
        left[...] = blend(left[...], left_gram)
        right[...] = blend(right[...], right_gram)
        pltpu.make_async_copy(left, left_out.at[1], sems.at[2]).start()
        pltpu.make_async_copy(right, right_out.at[1], sems.at[3]).start()

    for number, (source, target) in enumerate(
        [(left_done, left_out.at[0]), (right_done, right_out.at[0])]
        + [(left_done, left_out.at[1]), (right_done, right_out.at[1])]
    ):
        pltpu.make_async_copy(source, target, sems.at[number]).wait()


def settle(choice, gradient_back, left_state, right_state, left_done, right_done):
    slots, width, _ = left_state.shape
    both = pltpu.HBM(left_state.shape, jnp.bfloat16)
    return pl.pallas_call(
        settle_kernel,
        out_shape=(both, both),
        in_specs=[pl.BlockSpec(memory_space=pltpu.SMEM)]
        + [pl.BlockSpec(memory_space=pl.ANY)] * 5,
        out_specs=[pl.BlockSpec(memory_space=pltpu.HBM)] * 2,
        scratch_shapes=[pltpu.VMEM((width, width), jnp.bfloat16)] * 3
        + [pltpu.SemaphoreType.DMA((5,))],
        compiler_params=pltpu.CompilerParams(vmem_limit_bytes=VMEM_LIMIT),
        cost_estimate=pl.CostEstimate(
            flops=4 * width**3, bytes_accessed=16 * width**2, transcendentals=0
        ),
        name="settle_slots",
    )(choice, gradient_back, left_state, right_state, left_done, right_done)


def reorder_kernel(order, source, *rest):
    result, sem = rest[-2:]

    def move(number, carry):
        pltpu.make_async_copy(source.at[order[number]], result.at[number], sem).start()
        return carry

    lax.fori_loop(0, result.shape[0], move, 0, unroll=8)
    pltpu.make_async_copy(source, result, sem).wait()


def reorder(array, order, *needed):
    return pl.pallas_call(
        reorder_kernel,
        out_shape=pltpu.HBM(array.shape, array.dtype),
        in_specs=[pl.BlockSpec(memory_space=pltpu.SMEM)]
        + [pl.BlockSpec(memory_space=pl.ANY)] * (1 + len(needed)),
        out_specs=pl.BlockSpec(memory_space=pltpu.HBM),
        scratch_shapes=[pltpu.SemaphoreType.DMA],
        compiler_params=pltpu.CompilerParams(vmem_limit_bytes=VMEM_LIMIT // 4),
        name="reorder",
    )(order, array, *needed)


def late_loan_kernel(left_own, right_own, result, held, sems):
    width = right_own.shape[1]
    rest = held.shape[0] - width
    loads = [
        pltpu.make_async_copy(
            left_own.at[1, width - rest :], held.at[:rest], sems.at[0]
        ),
        pltpu.make_async_copy(right_own.at[1], held.at[rest:], sems.at[1]),
    ]
    for load in loads:
        load.start()
    for load in loads:
        load.wait()
    store = pltpu.make_async_copy(held, result, sems.at[2])
    store.start()
    store.wait()


def late_loan(left_state, right_state, early):
    width = left_state.shape[1]
    shape = (2 * width - early, width)
    return pl.pallas_call(
        late_loan_kernel,
        out_shape=pltpu.HBM(shape, jnp.bfloat16),
        in_specs=[pl.BlockSpec(memory_space=pl.ANY)] * 2,
        out_specs=pl.BlockSpec(memory_space=pltpu.HBM),
        scratch_shapes=[pltpu.VMEM(shape, jnp.bfloat16), pltpu.SemaphoreType.DMA((3,))],
        compiler_params=pltpu.CompilerParams(vmem_limit_bytes=VMEM_LIMIT // 4),
        name="late_loan",
    )(left_state, right_state)


def exchange_order(order, count):
    if len(order) != count:
        order = tuple(range(count))
    places = [order.index(device) for device in range(count)]
    return [list(order)], places


def pick(array, order):
    return array.at[order].get(mode="promise_in_bounds", unique_indices=True)


def local(grads, left_state, right_state, block_owner):
    rep_count = lax.axis_size("rep")
    fsdp_count = lax.axis_size("fsdp")
    group_index = lax.axis_index("rep")
    place_index = lax.axis_index("fsdp")
    held_blocks, shard_rows, block_width = grads.shape
    column_share = held_blocks // rep_count
    slot_count = left_state.shape[0]
    half = fsdp_count // 2
    swap = [(place, place ^ half) for place in range(fsdp_count)]
    positions = jnp.arange(held_blocks, dtype=jnp.int32)

    early = EARLY_ROWS
    lent_early = lax.ppermute(left_state[1, :early], "fsdp", swap)
    lent_late = lax.ppermute(late_loan(left_state, right_state, early), "fsdp", swap)

    rep_groups, rep_place = exchange_order(REP_ORDER, rep_count)
    fsdp_order = list(range(fsdp_count))
    first = FSDP_FIRST % fsdp_count
    fsdp_order[0], fsdp_order[first] = first, 0
    owner_table = block_owner.reshape(rep_count, held_blocks)
    owner_column = owner_table // slot_count % rep_count
    before = positions[None, :] < positions[:, None]

    my_column = lax.dynamic_index_in_dim(owner_column, group_index, 0, keepdims=False)
    alike = (my_column[:, None] == my_column[None, :]) & before
    my_place = sum(jnp.where(my_column == c, rep_place[c], 0) for c in range(rep_count))
    my_order = my_place * column_share + jnp.sum(alike.astype(jnp.int32), axis=1)
    my_picked = jnp.sum(
        jnp.where(my_order[None, :] == positions[:, None], positions[None, :], 0), axis=1
    )
    arrived = lax.all_to_all(
        pick(grads, my_picked),
        "rep", split_axis=0, concat_axis=0, tiled=True,
        axis_index_groups=rep_groups,
    )

    arrival_table = jnp.stack([owner_table[group] for group in rep_groups[0]])
    mine = arrival_table // slot_count % rep_count == group_index
    rank = jnp.sum((mine[:, None, :] & before[None]).astype(jnp.int32), axis=2)
    shares = jnp.arange(column_share, dtype=jnp.int32)
    taken = mine[:, None, :] & (rank[:, None, :] == shares[None, :, None])
    entry_owner = jnp.sum(jnp.where(taken, arrival_table[:, None, :], 0), axis=2).reshape(-1)

    sibling = jnp.any(entry_owner[None, :] == entry_owner[:, None] - 1, axis=1)
    second = (entry_owner % slot_count == 1) & sibling
    owner_place = entry_owner // (slot_count * rep_count)
    worker = jnp.where(second, owner_place ^ half, owner_place)
    worker_place = jnp.where(
        worker == 0, first, jnp.where(worker == first, 0, worker)
    )
    source_entry = jnp.sum(
        jnp.where(worker_place[None, :] == positions[:, None], positions[None, :], 0), axis=1
    )
    gradient = lax.all_to_all(
        reorder(arrived, source_entry, lent_early),
        "fsdp", split_axis=0, concat_axis=0, tiled=True,
        axis_index_groups=[fsdp_order],
    )

    first_slot = (place_index * rep_count + group_index) * slot_count
    owns_first = jnp.any(entry_owner == first_slot)
    owns_second = jnp.any(entry_owner == first_slot + 1)
    lent = ~(owns_first | owns_second)
    choice = jnp.stack([lent, ~owns_first, owns_first, owns_second]).astype(jnp.int32)
    update_block, left_done, right_done, gradient = work_on_block(
        fsdp_order, choice, gradient, left_state, right_state, lent_early, lent_late
    )

    returned_rows = lax.all_to_all(
        update_block,
        "fsdp", split_axis=0, concat_axis=0, tiled=True,
        axis_index_groups=[fsdp_order],
    )
    gradient_back = lax.ppermute(gradient, "fsdp", swap)
    left_new, right_new = settle(
        choice, gradient_back, left_state, right_state, left_done, right_done
    )
    at_home = lax.all_to_all(
        reorder(returned_rows, worker_place), "rep", split_axis=0, concat_axis=0, tiled=True,
        axis_index_groups=rep_groups
    )
    update = reorder(at_home, my_order)
    return (update, left_new, right_new)


def solution(mesh):
    return jax.shard_map(
        local,
        mesh=mesh,
        in_specs=(
            P("rep", "fsdp", None),
            P(("fsdp", "rep"), None, None),
            P(("fsdp", "rep"), None, None),
            P(),
        ),
        out_specs=(
            P("rep", "fsdp", None),
            P(("fsdp", "rep"), None, None),
            P(("fsdp", "rep"), None, None),
        ),
        check_vma=False,
    )
```

```python
import functools

import jax
import jax.numpy as jnp
from jax import lax
from jax.experimental import pallas as pl
from jax.experimental.pallas import tpu as pltpu
from jax.sharding import PartitionSpec as P

ITERS = 2
DECAY_RATE = 0.95
VMEM_LIMIT = 32 * 1024 * 1024
EARLY_ROWS = 448
REP_ORDER = (5, 1, 0, 7, 3, 4, 2, 6)
FSDP_FIRST = 42


def multiply(first, second):
    return jnp.dot(first, second, preferred_element_type=jnp.float32)


def inverse_root(stored):
    factor = stored.astype(jnp.float32)
    scaling = 2.5 / jnp.sqrt(jnp.sum(factor * factor))
    current = scaling * factor
    width = factor.shape[0]
    rows = lax.broadcasted_iota(jnp.int32, (width, width), 0)
    columns = lax.broadcasted_iota(jnp.int32, (width, width), 1)
    five = jnp.where(rows == columns, 5.0, 0.0)
    result = None
    for iteration in range(ITERS):
        tangent = ((five - current) * 0.25).astype(jnp.bfloat16)
        if iteration == 0:
            result = tangent
        else:
            result = multiply(result, tangent).astype(jnp.bfloat16)
        if iteration + 1 < ITERS:
            square = multiply(tangent, tangent).astype(jnp.bfloat16)
            fourth = multiply(square, square).astype(jnp.bfloat16)
            current = multiply(fourth, current.astype(jnp.bfloat16))
    return result


def grams(gradient):
    left = lax.dot_general(
        gradient, gradient, (((1,), (1,)), ((), ())), preferred_element_type=jnp.float32
    )
    right = lax.dot_general(
        gradient, gradient, (((0,), (0,)), ((), ())), preferred_element_type=jnp.float32
    )
    return left, right


def blend(old, gram):
    return (
        DECAY_RATE * old.astype(jnp.float32) + (1.0 - DECAY_RATE) * gram
    ).astype(jnp.bfloat16)


def block_kernel(
    order, choice, shares_ref, left_own, right_own, lent_early, lent_late,
    update_out, left_out, right_out, gradient_out,
    left_old, right_old, left_new, right_new, gradient_ref, update,
    old_sems, out_sems, update_sems,
):
    rows = shares_ref.shape[1]
    lent, slot = choice[0], choice[1]
    width = left_old.shape[0]
    early = lent_early.shape[0]

    @pl.when(lent == 1)
    def _():
        pltpu.make_async_copy(lent_early, left_old.at[:early], old_sems.at[0]).start()
        pltpu.make_async_copy(
            lent_late.at[: width - early], left_old.at[early:], old_sems.at[1]
        ).start()
        pltpu.make_async_copy(
            lent_late.at[width - early :], right_old, old_sems.at[2]
        ).start()

    @pl.when(lent == 0)
    def _():
        pltpu.make_async_copy(
            left_own.at[slot, :early], left_old.at[:early], old_sems.at[0]
        ).start()
        pltpu.make_async_copy(
            left_own.at[slot, early:], left_old.at[early:], old_sems.at[1]
        ).start()
        pltpu.make_async_copy(right_own.at[slot], right_old, old_sems.at[2]).start()

    for number, place in enumerate(order):
        gradient_ref[place * rows : (place + 1) * rows, :] = shares_ref[number]
    keep_gradient = pltpu.make_async_copy(gradient_ref, gradient_out, out_sems.at[2])
    keep_gradient.start()
    pltpu.make_async_copy(lent_early, left_old.at[:early], old_sems.at[0]).wait()
    pltpu.make_async_copy(
        lent_late.at[: width - early], left_old.at[early:], old_sems.at[1]
    ).wait()
    pltpu.make_async_copy(lent_late.at[width - early :], right_old, old_sems.at[2]).wait()
    gradient = gradient_ref[...]
    left_gram, right_gram = grams(gradient)
    left_factor = blend(left_old[...], left_gram)
    right_factor = blend(right_old[...], right_gram)
    left_new[...] = left_factor
    right_new[...] = right_factor
    keep_left = pltpu.make_async_copy(left_new, left_out, out_sems.at[0])
    keep_right = pltpu.make_async_copy(right_new, right_out, out_sems.at[1])
    keep_left.start()
    keep_right.start()
    left_root = inverse_root(left_factor)
    right_root = inverse_root(right_factor)
    half_product = multiply(left_root, gradient).astype(jnp.bfloat16)
    raw_update = multiply(half_product, right_root)
    wide = gradient.astype(jnp.float32)
    grad_norm = jnp.sqrt(jnp.sum(wide * wide))
    raw_norm = jnp.sqrt(jnp.sum(raw_update * raw_update))
    scale = grad_norm / (raw_norm + 1e-06)
    sends = []
    part = len(order) // update_sems.shape[0]
    for number in range(update_sems.shape[0]):
        shares = slice(number * part, (number + 1) * part)
        for share in range(number * part, (number + 1) * part):
            place = order[share]
            piece = raw_update[place * rows : (place + 1) * rows, :]
            update[share] = (piece * scale).astype(jnp.bfloat16)
        send = pltpu.make_async_copy(
            update.at[shares], update_out.at[shares], update_sems.at[number]
        )
        send.start()
        sends.append(send)
    for send in [keep_gradient, keep_left, keep_right] + sends:
        send.wait()


def work_on_block(
    order, choice, shares, left_state, right_state, lent_early, lent_late
):
    width = shares.shape[2]
    square = pltpu.HBM((width, width), jnp.bfloat16)
    return pl.pallas_call(
        functools.partial(block_kernel, order),
        out_shape=(pltpu.HBM(shares.shape, jnp.bfloat16),) + (square,) * 3,
        in_specs=[
            pl.BlockSpec(memory_space=pltpu.SMEM),
            pl.BlockSpec(memory_space=pltpu.VMEM),
        ]
        + [pl.BlockSpec(memory_space=pl.ANY)] * 4,
        out_specs=[pl.BlockSpec(memory_space=pltpu.HBM)] * 4,
        scratch_shapes=[pltpu.VMEM((width, width), jnp.bfloat16)] * 5
        + [pltpu.VMEM(shares.shape, jnp.bfloat16)]
        + [pltpu.SemaphoreType.DMA((3,)), pltpu.SemaphoreType.DMA((3,)), pltpu.SemaphoreType.DMA((4,))],
        compiler_params=pltpu.CompilerParams(vmem_limit_bytes=VMEM_LIMIT),
        cost_estimate=pl.CostEstimate(
            flops=24 * width**3, bytes_accessed=12 * width**2, transcendentals=0
        ),
        name="block_step",
    )(choice, shares, left_state, right_state, lent_early, lent_late)


def settle_kernel(
    choice, gradient_back, left_own, right_own, left_done, right_done, left_out, right_out,
    gradient, left, right, sems,
):
    has_first, has_second = choice[2] == 1, choice[3] == 1
    has_both = has_first & has_second

    @pl.when(has_first)
    def _():
        pltpu.make_async_copy(left_done, left_out.at[0], sems.at[0]).start()
        pltpu.make_async_copy(right_done, right_out.at[0], sems.at[1]).start()

    @pl.when(~has_first)
    def _():
        pltpu.make_async_copy(left_own.at[0], left_out.at[0], sems.at[0]).start()
        pltpu.make_async_copy(right_own.at[0], right_out.at[0], sems.at[1]).start()

    @pl.when(has_second & ~has_first)
    def _():
        pltpu.make_async_copy(left_done, left_out.at[1], sems.at[2]).start()
        pltpu.make_async_copy(right_done, right_out.at[1], sems.at[3]).start()

    @pl.when(~has_second)
    def _():
        pltpu.make_async_copy(left_own.at[1], left_out.at[1], sems.at[2]).start()
        pltpu.make_async_copy(right_own.at[1], right_out.at[1], sems.at[3]).start()

    @pl.when(has_both)
    def _():
        loads = [
            pltpu.make_async_copy(left_own.at[1], left, sems.at[2]),
            pltpu.make_async_copy(right_own.at[1], right, sems.at[3]),
            pltpu.make_async_copy(gradient_back, gradient, sems.at[4]),
        ]
        for load in loads:
            load.start()
        for load in loads:
            load.wait()
        left_gram, right_gram = grams(gradient[...])
        left[...] = blend(left[...], left_gram)
        right[...] = blend(right[...], right_gram)
        pltpu.make_async_copy(left, left_out.at[1], sems.at[2]).start()
        pltpu.make_async_copy(right, right_out.at[1], sems.at[3]).start()

    for number, (source, target) in enumerate(
        [(left_done, left_out.at[0]), (right_done, right_out.at[0])]
        + [(left_done, left_out.at[1]), (right_done, right_out.at[1])]
    ):
        pltpu.make_async_copy(source, target, sems.at[number]).wait()


def settle(choice, gradient_back, left_state, right_state, left_done, right_done):
    slots, width, _ = left_state.shape
    both = pltpu.HBM(left_state.shape, jnp.bfloat16)
    return pl.pallas_call(
        settle_kernel,
        out_shape=(both, both),
        in_specs=[pl.BlockSpec(memory_space=pltpu.SMEM)]
        + [pl.BlockSpec(memory_space=pl.ANY)] * 5,
        out_specs=[pl.BlockSpec(memory_space=pltpu.HBM)] * 2,
        scratch_shapes=[pltpu.VMEM((width, width), jnp.bfloat16)] * 3
        + [pltpu.SemaphoreType.DMA((5,))],
        compiler_params=pltpu.CompilerParams(vmem_limit_bytes=VMEM_LIMIT),
        cost_estimate=pl.CostEstimate(
            flops=4 * width**3, bytes_accessed=16 * width**2, transcendentals=0
        ),
        name="settle_slots",
    )(choice, gradient_back, left_state, right_state, left_done, right_done)


def reorder_kernel(order, source, *rest):
    result, sem = rest[-2:]

    def move(number, carry):
        pltpu.make_async_copy(source.at[order[number]], result.at[number], sem).start()
        return carry

    lax.fori_loop(0, result.shape[0], move, 0, unroll=8)
    pltpu.make_async_copy(source, result, sem).wait()


def reorder(array, order, *needed):
    return pl.pallas_call(
        reorder_kernel,
        out_shape=pltpu.HBM(array.shape, array.dtype),
        in_specs=[pl.BlockSpec(memory_space=pltpu.SMEM)]
        + [pl.BlockSpec(memory_space=pl.ANY)] * (1 + len(needed)),
        out_specs=pl.BlockSpec(memory_space=pltpu.HBM),
        scratch_shapes=[pltpu.SemaphoreType.DMA],
        compiler_params=pltpu.CompilerParams(vmem_limit_bytes=VMEM_LIMIT // 4),
        name="reorder",
    )(order, array, *needed)


def late_loan_kernel(left_own, right_own, result, held, sems):
    width = right_own.shape[1]
    rest = held.shape[0] - width
    loads = [
        pltpu.make_async_copy(
            left_own.at[1, width - rest :], held.at[:rest], sems.at[0]
        ),
        pltpu.make_async_copy(right_own.at[1], held.at[rest:], sems.at[1]),
    ]
    for load in loads:
        load.start()
    for load in loads:
        load.wait()
    store = pltpu.make_async_copy(held, result, sems.at[2])
    store.start()
    store.wait()


def late_loan(left_state, right_state, early):
    width = left_state.shape[1]
    shape = (2 * width - early, width)
    return pl.pallas_call(
        late_loan_kernel,
        out_shape=pltpu.HBM(shape, jnp.bfloat16),
        in_specs=[pl.BlockSpec(memory_space=pl.ANY)] * 2,
        out_specs=pl.BlockSpec(memory_space=pltpu.HBM),
        scratch_shapes=[pltpu.VMEM(shape, jnp.bfloat16), pltpu.SemaphoreType.DMA((3,))],
        compiler_params=pltpu.CompilerParams(vmem_limit_bytes=VMEM_LIMIT // 4),
        name="late_loan",
    )(left_state, right_state)


def exchange_order(order, count):
    if len(order) != count:
        order = tuple(range(count))
    places = [order.index(device) for device in range(count)]
    return [list(order)], places


def pick(array, order):
    return array.at[order].get(mode="promise_in_bounds", unique_indices=True)


def local(grads, left_state, right_state, block_owner):
    rep_count = lax.axis_size("rep")
    fsdp_count = lax.axis_size("fsdp")
    group_index = lax.axis_index("rep")
    place_index = lax.axis_index("fsdp")
    held_blocks, shard_rows, block_width = grads.shape
    column_share = held_blocks // rep_count
    slot_count = left_state.shape[0]
    half = fsdp_count // 2
    swap = [(place, place ^ half) for place in range(fsdp_count)]
    positions = jnp.arange(held_blocks, dtype=jnp.int32)

    early = EARLY_ROWS
    lent_early = lax.ppermute(left_state[1, :early], "fsdp", swap)
    lent_late = lax.ppermute(late_loan(left_state, right_state, early), "fsdp", swap)

    rep_groups, rep_place = exchange_order(REP_ORDER, rep_count)
    fsdp_order = list(range(fsdp_count))
    first = FSDP_FIRST % fsdp_count
    fsdp_order[0], fsdp_order[first] = first, 0
    owner_table = block_owner.reshape(rep_count, held_blocks)
    owner_column = owner_table // slot_count % rep_count
    before = positions[None, :] < positions[:, None]

    my_column = lax.dynamic_index_in_dim(owner_column, group_index, 0, keepdims=False)
    alike = (my_column[:, None] == my_column[None, :]) & before
    my_place = sum(jnp.where(my_column == c, rep_place[c], 0) for c in range(rep_count))
    my_order = my_place * column_share + jnp.sum(alike.astype(jnp.int32), axis=1)
    my_picked = jnp.sum(
        jnp.where(my_order[None, :] == positions[:, None], positions[None, :], 0), axis=1
    )
    arrived = lax.all_to_all(
        pick(grads, my_picked),
        "rep", split_axis=0, concat_axis=0, tiled=True,
        axis_index_groups=rep_groups,
    )

    arrival_table = jnp.stack([owner_table[group] for group in rep_groups[0]])
    mine = arrival_table // slot_count % rep_count == group_index
    rank = jnp.sum((mine[:, None, :] & before[None]).astype(jnp.int32), axis=2)
    shares = jnp.arange(column_share, dtype=jnp.int32)
    taken = mine[:, None, :] & (rank[:, None, :] == shares[None, :, None])
    entry_owner = jnp.sum(jnp.where(taken, arrival_table[:, None, :], 0), axis=2).reshape(-1)

    sibling = jnp.any(entry_owner[None, :] == entry_owner[:, None] - 1, axis=1)
    second = (entry_owner % slot_count == 1) & sibling
    owner_place = entry_owner // (slot_count * rep_count)
    worker = jnp.where(second, owner_place ^ half, owner_place)
    worker_place = jnp.where(
        worker == 0, first, jnp.where(worker == first, 0, worker)
    )
    source_entry = jnp.sum(
        jnp.where(worker_place[None, :] == positions[:, None], positions[None, :], 0), axis=1
    )
    gradient = lax.all_to_all(
        reorder(arrived, source_entry, lent_early),
        "fsdp", split_axis=0, concat_axis=0, tiled=True,
        axis_index_groups=[fsdp_order],
    )

    first_slot = (place_index * rep_count + group_index) * slot_count
    owns_first = jnp.any(entry_owner == first_slot)
    owns_second = jnp.any(entry_owner == first_slot + 1)
    lent = ~(owns_first | owns_second)
    choice = jnp.stack([lent, ~owns_first, owns_first, owns_second]).astype(jnp.int32)
    update_block, left_done, right_done, gradient = work_on_block(
        fsdp_order, choice, gradient, left_state, right_state, lent_early, lent_late
    )

    returned_rows = lax.all_to_all(
        update_block,
        "fsdp", split_axis=0, concat_axis=0, tiled=True,
        axis_index_groups=[fsdp_order],
    )
    gradient_back = lax.ppermute(gradient, "fsdp", swap)
    left_new, right_new = settle(
        choice, gradient_back, left_state, right_state, left_done, right_done
    )
    at_home = lax.all_to_all(
        reorder(returned_rows, worker_place), "rep", split_axis=0, concat_axis=0, tiled=True,
        axis_index_groups=rep_groups
    )
    update = reorder(at_home, my_order)
    return (update, left_new, right_new)


def solution(mesh):
    return jax.shard_map(
        local,
        mesh=mesh,
        in_specs=(
            P("rep", "fsdp", None),
            P(("fsdp", "rep"), None, None),
            P(("fsdp", "rep"), None, None),
            P(),
        ),
        out_specs=(
            P("rep", "fsdp", None),
            P(("fsdp", "rep"), None, None),
            P(("fsdp", "rep"), None, None),
        ),
        check_vma=False,
    )
```
